32 devices in a mesh: dp: 4 (over y, x), ctx: 8 (over z, core).
Axes of the slice: x: 2, y: 2, z: 4, core: 2. Of those that a mesh axis runs over, the one named last changes fastest.
Arguments:
- tokens: bfloat16 [8, 1024, 1024], P('dp', 'ctx'), may hold values from -6 to 6
- cotangent: bfloat16 [8, 1024, 1024], P('dp', 'ctx'), may hold values from -6 to 6
- segments: int32 [8, 1024], P('dp'), may hold values from 0 to 7, as said below
- span_order: int32 [8], replicated, may hold values from 0 to 7, each once
- w_query: bfloat16 [1024, 2048], P(('dp', 'ctx')), may hold values from -0.1875 to 0.1875
- key_weight: bfloat16 [1024, 1024], P(('dp', 'ctx')), may hold values from -0.1875 to 0.1875
- value_weight: bfloat16 [1024, 1024], P(('dp', 'ctx')), may hold values from -0.1875 to 0.1875
- w_output: bfloat16 [2048, 1024], P(('dp', 'ctx')), may hold values from -0.5 to 0.5
- w_gate: bfloat16 [1024, 3072], P(('dp', 'ctx')), may hold values from -0.1875 to 0.1875
- w_up: bfloat16 [1024, 3072], P(('dp', 'ctx')), may hold values from -0.1875 to 0.1875
- w_down: bfloat16 [3072, 1024], P(('dp', 'ctx')), may hold values from -0.109375 to 0.109375
- gains: bfloat16 [2304], P(('dp', 'ctx')), may hold values from 0.25 to 1.75
Outputs:
- result: bfloat16 [8, 1024, 1024], P('dp', 'ctx')
- input_grad: float32 [8, 1024, 1024], P('dp', 'ctx')
- grad_query: float32 [1024, 2048], P(('dp', 'ctx'))
- grad_key: float32 [1024, 1024], P(('dp', 'ctx'))
- grad_value: float32 [1024, 1024], P(('dp', 'ctx'))
- grad_output: float32 [2048, 1024], P(('dp', 'ctx'))
- grad_gate: float32 [1024, 3072], P(('dp', 'ctx'))
- grad_up: float32 [1024, 3072], P(('dp', 'ctx'))
- grad_down: float32 [3072, 1024], P(('dp', 'ctx'))
- grad_gains: float32 [2304], P(('dp', 'ctx'))
The draws below stay inside these ranges and needn't reach their ends.
Inputs may be any that keep to these rules, and one draw needn't show every extreme that they name: `segments`: along each sequence the numbers start at 0 and rise by 0 or 1 from one position to the next; a run of equal numbers is one document. `span_order`: each slot number appears once.
All inputs are finite; a program needn't handle non-finite values.
Results may differ from the reference program's by a relative error of at most 0.015.
Values may be sent and summed in bfloat16 or wider, within the bound.
A program may use at most 256 MiB of HBM per device.

```python
import math
import jax
import jax.numpy as jnp
from jax import lax

MODEL_WIDTH = 1024
QUERY_HEADS = 16
KEY_VALUE_HEADS = 8
HEAD_SIZE = 128
FF = 3072
SEQUENCE_LENGTH = 1024
SEQS_DEV = 2
SEQS = 8
SPAN = 128
GAINS = 2304
N_CTX = 8


def draw_segments(key, part):
    key = jax.random.fold_in(key, 11)
    key_rolls, key_rows = jax.random.split(key)
    spacing = max(SEQUENCE_LENGTH // 4, 2)
    rolls = jax.random.randint(key_rolls, (SEQS, SEQUENCE_LENGTH), 0, spacing)
    spots = jnp.arange(SEQUENCE_LENGTH)
    forced = spots % (SEQUENCE_LENGTH // 8) == 0
    chosen = jax.random.randint(key_rows, (SEQS // SEQS_DEV, 1), 0, SEQS_DEV)
    row_place = (jnp.arange(SEQS) % SEQS_DEV).reshape(SEQS // SEQS_DEV, SEQS_DEV)
    long_row = (row_place == chosen).reshape(SEQS, 1)
    inner = (spots >= SPAN // 2) & (spots < SEQUENCE_LENGTH - SPAN // 2)
    opens = (rolls == 0) | (spots == 0)[None, :] | forced[None, :] & jnp.logical_not(long_row)
    opens = opens & jnp.logical_not(long_row & inner[None, :])
    counted = jnp.cumsum(opens.astype(jnp.int32), axis=1) - 1
    return jnp.minimum(counted, 7).astype(jnp.int32)


def block_levels(stream_key, extent, cuts, smallest, high):
    factor_of, own = 1.0, jax.random.fold_in(stream_key, 6)
    for axis_at, shards_of in cuts:
        draws = jnp.exp(jax.random.uniform(jax.random.fold_in(own, axis_at), (shards_of,), jnp.float32, smallest / len(cuts), high / len(cuts)))
        factor_of = factor_of * jnp.repeat(draws, extent[axis_at] // shards_of).reshape([-1 if axis == axis_at else 1 for axis in range(len(extent))])
    return factor_of


def normal_values(key, shape, spread, limit, shards=(), kind=jnp.bfloat16):
    entries = jax.random.normal(key, shape, jnp.float32) * spread
    if len(shards) > 0:
        entries = block_levels(key, shape, shards, -0.22, 0.18) * entries
    return jnp.clip(entries, min=-limit, max=limit).astype(kind)


def setup_inputs(seed: int = 0) -> dict:
    key_list = jax.random.split(jax.random.key(seed), 13)
    tokens = normal_values(key_list[0], (SEQS, SEQUENCE_LENGTH, MODEL_WIDTH), 1.0, 6.0, ((0, 4), (1, 8)))
    cotangent = normal_values(key_list[1], (SEQS, SEQUENCE_LENGTH, MODEL_WIDTH), 1.0, 6.0, ((0, 4), (1, 8)))
    segments = draw_segments(jax.random.fold_in(key_list[12], 71), 0)
    span_order = jax.random.permutation(key_list[3], N_CTX).astype(jnp.int32)
    w_query = normal_values(key_list[4], (MODEL_WIDTH, QUERY_HEADS * HEAD_SIZE), MODEL_WIDTH ** -0.5, 0.1875, ((0, 32),))
    key_weight = normal_values(key_list[5], (MODEL_WIDTH, KEY_VALUE_HEADS * HEAD_SIZE), MODEL_WIDTH ** -0.5, 0.1875, ((0, 32),))
    value_weight = normal_values(key_list[6], (MODEL_WIDTH, KEY_VALUE_HEADS * HEAD_SIZE), MODEL_WIDTH ** -0.5, 0.1875, ((0, 32),))
    w_output = normal_values(key_list[7], (QUERY_HEADS * HEAD_SIZE, MODEL_WIDTH), (QUERY_HEADS * HEAD_SIZE // 16) ** -0.5, 0.5, ((0, 32),))
    w_gate = normal_values(key_list[8], (MODEL_WIDTH, FF), MODEL_WIDTH ** -0.5, 0.1875, ((0, 32),))
    w_up = normal_values(key_list[9], (MODEL_WIDTH, FF), MODEL_WIDTH ** -0.5, 0.1875, ((0, 32),))
    w_down = normal_values(key_list[10], (FF, MODEL_WIDTH), FF ** -0.5, 0.109375, ((0, 32),))
    gains = jnp.clip(1.0 + 0.15 * jax.random.normal(key_list[11], (GAINS,), jnp.float32), 0.25, 1.75).astype(jnp.bfloat16)
    return {"tokens": tokens, "cotangent": cotangent, "segments": segments, "span_order": span_order, "w_query": w_query, "key_weight": key_weight, "value_weight": value_weight, "w_output": w_output, "w_gate": w_gate, "w_up": w_up, "w_down": w_down, "gains": gains}


norm_eps = 1e-06
rope_base = 1000000.0
masked_score = -1e+30

@jax.custom_vjp
def lower_precision(v):
    return lax.optimization_barrier(v.astype(jnp.bfloat16)).astype(jnp.float32)

@jax.custom_vjp
def lower_precision_gradient(v):
    return v

def low_keep(v):
    return (lower_precision(v), None)

def low_pass(kept, grad):
    return (grad,)

def back_keep(v):
    return (v, None)

def back_low(kept, grad):
    return (lower_precision(grad),)
lower_precision.defvjp(low_keep, low_pass)
lower_precision_gradient.defvjp(back_keep, back_low)

def rms_scale(value_rows, gain):
    return value_rows * lax.rsqrt(lax.optimization_barrier(jnp.mean(value_rows * value_rows, axis=-1, keepdims=True)) + norm_eps) * gain

def rotate(value_rows, positions):
    half = value_rows.shape[-1] // 2
    freq = rope_base ** (-(jnp.arange(half).astype(jnp.float32) * 2.0 / value_rows.shape[-1]))
    angle = positions.astype(jnp.float32)[:, None] * freq[None, :]
    cosine = jnp.cos(angle)[:, None, :]
    sine = jnp.sin(angle)[:, None, :]
    first_half = value_rows[..., :half]
    second_half = value_rows[..., half:]
    return jnp.concatenate([first_half * cosine - second_half * sine, second_half * cosine + first_half * sine], axis=-1)

def token_layout(segments, span_order, token_span):
    row_count, segment_length = segments.shape
    spots = jnp.arange(segment_length, dtype=jnp.int32)
    opens = jnp.concatenate([jnp.ones((row_count, 1), dtype=jnp.bool_), segments[:, 1:] != segments[:, :-1]], axis=1)
    firsts = lax.cummax(jnp.where(opens, spots[None, :], jnp.int32(0)), axis=1)
    in_doc = (spots[None, :] - firsts).astype(jnp.int32)
    true_index = (span_order[:, None] * token_span + jnp.arange(token_span, dtype=jnp.int32)[None, :]).reshape(segment_length).astype(jnp.int32)
    return (true_index, jnp.take(segments, true_index, axis=1), jnp.take(in_doc, true_index, axis=1))

def matrix_product(left, right):
    return jnp.dot(left, right, preferred_element_type=jnp.float32, precision=lax.Precision.HIGHEST)

def swiglu(gate, up_part):
    return gate * jax.nn.sigmoid(gate) * up_part

def layer(inputs, weights, seg_row, pos_row, true_index):
    w_query, key_weight, value_weight, w_output, w_gate, w_up, w_down, gain_all = weights
    gain_one = gain_all[:MODEL_WIDTH]
    gain_two = gain_all[MODEL_WIDTH:2 * MODEL_WIDTH]
    gain_query = gain_all[2 * MODEL_WIDTH:2 * MODEL_WIDTH + HEAD_SIZE]
    gain_key = gain_all[2 * MODEL_WIDTH + HEAD_SIZE:]
    score_scale = 1.0 / math.sqrt(HEAD_SIZE)
    first_normed = lower_precision(rms_scale(inputs, gain_one))
    q_lin = lower_precision_gradient(matrix_product(first_normed, w_query)).reshape(SEQUENCE_LENGTH, QUERY_HEADS, HEAD_SIZE)
    key_linear = lower_precision_gradient(matrix_product(first_normed, key_weight)).reshape(SEQUENCE_LENGTH, KEY_VALUE_HEADS, HEAD_SIZE)
    value_rows = lower_precision_gradient(lower_precision(matrix_product(first_normed, value_weight))).reshape(SEQUENCE_LENGTH, KEY_VALUE_HEADS, HEAD_SIZE)
    query_rows = lower_precision(rotate(rms_scale(q_lin, gain_query), pos_row))
    keys = lower_precision(rotate(rms_scale(key_linear, gain_key), pos_row))
    rows_per_block = min(512, SEQUENCE_LENGTH)
    block_count = SEQUENCE_LENGTH // rows_per_block

    def attend(items):
        query_block, index_block, seg_block = items
        grouped_queries = query_block.reshape(rows_per_block, KEY_VALUE_HEADS, QUERY_HEADS // KEY_VALUE_HEADS, HEAD_SIZE)
        scores = lower_precision_gradient(jnp.einsum('qhgd,khd->hgqk', grouped_queries, keys, precision=lax.Precision.HIGHEST) * score_scale)
        allowed = (seg_block[:, None] == seg_row[None, :]) & (true_index[None, :] <= index_block[:, None])
        scores = jnp.where(allowed[None, None], scores, masked_score)
        top = lax.optimization_barrier(jnp.max(scores, axis=-1, keepdims=True))
        expo = jnp.exp(scores - top)
        probs = lower_precision(expo / lax.optimization_barrier(jnp.sum(expo, axis=-1, keepdims=True)))
        mixed_block = jnp.einsum('hgqk,khd->qhgd', probs, value_rows, precision=lax.Precision.HIGHEST)
        return mixed_block.reshape(rows_per_block, QUERY_HEADS * HEAD_SIZE)
    mixed = lax.map(jax.checkpoint(attend), (query_rows.reshape(block_count, rows_per_block, QUERY_HEADS, HEAD_SIZE), true_index.reshape(block_count, rows_per_block), seg_row.reshape(block_count, rows_per_block)))
    mixed = lower_precision_gradient(lower_precision(mixed.reshape(SEQUENCE_LENGTH, QUERY_HEADS * HEAD_SIZE)))
    middle = inputs + lower_precision_gradient(matrix_product(mixed, w_output))
    normed_two = lower_precision(rms_scale(middle, gain_two))
    gate = lower_precision_gradient(matrix_product(normed_two, w_gate))
    up_part = lower_precision_gradient(matrix_product(normed_two, w_up))
    hidden = lower_precision(swiglu(gate, up_part))
    return middle + lower_precision_gradient(matrix_product(hidden, w_down))

def reference(tokens, cotangent, segments, span_order, w_query, key_weight, value_weight, w_output, w_gate, w_up, w_down, gains):
    token_span = SEQUENCE_LENGTH // N_CTX
    true_index, seg_store, pos_store = token_layout(segments, span_order, token_span)
    weights = tuple((item.astype(jnp.float32) for item in (w_query, key_weight, value_weight, w_output, w_gate, w_up, w_down, gains)))

    def one_sequence(carry, items):
        inputs, grad_in, seg_row, pos_row = items

        def forward(inputs_now, *weights_now):
            return layer(inputs_now, weights_now, seg_row, pos_row, true_index)
        output, backward = jax.vjp(forward, inputs, *weights)
        grads = backward(grad_in)
        summed = tuple((accum + piece for accum, piece in zip(carry, grads[1:])))
        return (summed, (output.astype(jnp.bfloat16), grads[0]))
    start = tuple((jnp.zeros(item.shape, jnp.float32) for item in weights))
    totals, (outputs, input_grads) = lax.scan(one_sequence, start, (tokens.astype(jnp.float32), cotangent.astype(jnp.float32), seg_store, pos_store))
    return (outputs, input_grads, totals[0], totals[1], totals[2], totals[3], totals[4], totals[5], totals[6], totals[7])
```

```python
import math

import jax
import jax.numpy as jnp
from jax import lax
from jax.sharding import Mesh
from jax.sharding import PartitionSpec as P

QUERY_HEADS = 16
KEY_VALUE_HEADS = 8
HEAD_SIZE = 128


norm_eps = 1e-06
rope_base = 1000000.0
masked_score = -1e30


def rms_scale(value_rows, gain):
    return (
        value_rows
        * lax.rsqrt(jnp.mean(value_rows * value_rows, axis=-1, keepdims=True) + norm_eps)
        * gain
    )


def rotate(value_rows, positions):
    half = value_rows.shape[-1] // 2
    freq = rope_base ** (-(jnp.arange(half).astype(jnp.float32) * 2.0 / value_rows.shape[-1]))
    angle = positions.astype(jnp.float32)[:, None] * freq[None, :]
    cosine = jnp.cos(angle)[:, None, :]
    sine = jnp.sin(angle)[:, None, :]
    first_half = value_rows[..., :half]
    second_half = value_rows[..., half:]
    return jnp.concatenate(
        [first_half * cosine - second_half * sine, second_half * cosine + first_half * sine],
        axis=-1,
    )


def token_layout(segments, span_order, token_span):
    row_count, segment_length = segments.shape
    spots = jnp.arange(segment_length, dtype=jnp.int32)
    opens = jnp.concatenate(
        [jnp.ones((row_count, 1), dtype=jnp.bool_), segments[:, 1:] != segments[:, :-1]], axis=1
    )
    firsts = lax.cummax(jnp.where(opens, spots[None, :], jnp.int32(0)), axis=1)
    in_doc = spots[None, :] - firsts
    true_index = (
        span_order[:, None] * token_span + jnp.arange(token_span, dtype=jnp.int32)[None, :]
    ).reshape(segment_length)
    return (
        true_index,
        jnp.take(segments, true_index, axis=1),
        jnp.take(in_doc, true_index, axis=1),
    )


def swiglu(gate, up_part):
    return gate * jax.nn.sigmoid(gate) * up_part


SWAP = ((0, 1), (1, 0))


def swap(value):
    return lax.ppermute(value, "core", SWAP)


def local(
    tokens,
    cotangent,
    segments,
    span_order,
    w_query,
    key_weight,
    value_weight,
    w_output,
    w_gate,
    w_up,
    w_down,
    gains,
):
    sequence_count, token_span, width = tokens.shape
    token_rows = sequence_count * token_span
    group = QUERY_HEADS // KEY_VALUE_HEADS
    kv_width = KEY_VALUE_HEADS * HEAD_SIZE
    q_width = QUERY_HEADS * HEAD_SIZE
    core = lax.axis_index("core")
    first_core = core == 0
    chips = lax.axis_size("dp") * lax.axis_size("z")
    z_count = lax.axis_size("z")
    slot = lax.axis_index("z") * 2 + core
    f32, bf16 = jnp.float32, jnp.bfloat16

    def order(own, par, axis=-1):
        return jnp.concatenate(
            [jnp.where(first_core, own, par), jnp.where(first_core, par, own)], axis=axis
        )

    def halves(value):
        half = value.shape[-1] // 2
        a, b = value[..., :half], value[..., half:]
        return jnp.where(first_core, a, b), jnp.where(first_core, b, a)

    def chip_rows(parts):
        split = [halves(p) for p in parts]
        keep = jnp.concatenate([p[0] for p in split], axis=1)
        give = jnp.concatenate([p[1] for p in split], axis=1)
        return order(keep, swap(give), axis=0)

    def own_rows(value, sizes):
        rows = value.shape[0] // 2
        a, b = value[:rows], value[rows:]
        keep = jnp.where(first_core, a, b)
        got = swap(jnp.where(first_core, b, a))
        out, at = [], 0
        for size in sizes:
            out.append(order(keep[:, at : at + size], got[:, at : at + size]).astype(f32))
            at += size
        return out

    def gather(value):
        own = lax.all_gather(value, ("dp", "z"), axis=0, tiled=True)
        return own, swap(own)

    def scatter(own, par):
        total = (own + swap(par.astype(bf16)).astype(f32)).astype(bf16)
        return lax.psum_scatter(total, ("dp", "z"), scatter_dimension=0, tiled=True)

    def dot(a, b):
        return jnp.dot(a, b, preferred_element_type=f32)

    def dot_nt(a, b):
        return lax.dot_general(a, b, (((1,), (1,)), ((), ())), preferred_element_type=f32)

    def dot_tn(a, b):
        return lax.dot_general(a, b, (((0,), (0,)), ((), ())), preferred_element_type=f32)

    chip_qkv = chip_rows([w_query, key_weight, value_weight])
    chip_out = chip_rows([w_output])
    chip_gu = chip_rows([w_gate, w_up])
    chip_down = chip_rows([w_down])
    share = gains.shape[0]
    rows_chip = chip_qkv.shape[0]
    pad = jnp.pad(gains[None, :], ((0, rows_chip - 1), (0, 128 - share)))
    qkv_own, qkv_par = gather(jnp.concatenate([chip_qkv, pad], axis=1))
    lin_width = chip_qkv.shape[1]

    def gains_of(full):
        return full[::rows_chip, lin_width : lin_width + share]

    gain_all = order(gains_of(qkv_own)[:, None, :], gains_of(qkv_par)[:, None, :], axis=1)
    gain_all = gain_all.reshape(-1).astype(f32)
    gain_one = gain_all[:width]
    gain_two = gain_all[width : 2 * width]
    gain_query = gain_all[2 * width : 2 * width + HEAD_SIZE]
    gain_key = gain_all[2 * width + HEAD_SIZE :]

    true_index, seg_store, pos_store = token_layout(segments, span_order, token_span)
    query_index = lax.dynamic_slice_in_dim(true_index, slot * token_span, token_span, 0)
    query_segs = lax.dynamic_slice_in_dim(seg_store, slot * token_span, token_span, 1)
    query_pos = lax.dynamic_slice_in_dim(pos_store, slot * token_span, token_span, 1).reshape(
        token_rows
    )
    pairs_index = true_index.reshape(z_count, 2, token_span)
    key_index = order(pairs_index[:, 0], pairs_index[:, 1], axis=0).reshape(-1)
    pairs_segs = seg_store.reshape(sequence_count, z_count, 2, token_span)
    key_segs = order(pairs_segs[:, :, 0], pairs_segs[:, :, 1], axis=1).reshape(sequence_count, -1)
    allowed = (query_segs[:, :, None] == key_segs[:, None, :]) & (
        key_index[None, None, :] <= query_index[None, :, None]
    )

    def head_path(lin_part, gain):
        return rotate(rms_scale(lin_part, gain), query_pos)

    inputs = tokens.reshape(token_rows, width).astype(f32)
    first_normed = rms_scale(inputs, gain_one).astype(bf16)
    lin_own, lin_par = dot(first_normed, qkv_own), dot(first_normed, qkv_par)
    half_q, half_kv = q_width // 2, kv_width // 2

    def lin_slice(start, size):
        return order(lin_own[:, start : start + size], lin_par[:, start : start + size])

    q_lin = lin_slice(0, half_q).reshape(token_rows, QUERY_HEADS, HEAD_SIZE)
    key_linear = lin_slice(half_q, half_kv).reshape(token_rows, KEY_VALUE_HEADS, HEAD_SIZE)
    values_low = lin_slice(half_q + half_kv, half_kv).astype(bf16)
    query_rows = head_path(q_lin, gain_query).astype(bf16)
    keys = head_path(key_linear, gain_key).astype(bf16)

    kv = jnp.stack([keys.reshape(values_low.shape), values_low])
    kv = kv.reshape(2, sequence_count, token_span, KEY_VALUE_HEADS, HEAD_SIZE)
    kv = kv.transpose(0, 1, 3, 2, 4)
    kv_own = lax.all_gather(kv, "z", axis=0)
    kv_all = jnp.concatenate([kv_own, swap(kv_own)], axis=0)
    kv_all = kv_all.transpose(1, 2, 3, 0, 4, 5)
    key_count = kv_all.shape[3] * token_span
    kv_all = kv_all.reshape(2, sequence_count, KEY_VALUE_HEADS, key_count, HEAD_SIZE)
    k_all, v_all = kv_all[0], kv_all[1]

    out_own, out_par = gather(chip_out)
    gu_own, gu_par = gather(chip_gu)
    down_own, down_par = gather(chip_down)

    def to_heads(value):
        value = value.reshape(sequence_count, token_span, KEY_VALUE_HEADS, group, HEAD_SIZE)
        value = value.transpose(0, 2, 3, 1, 4)
        return value.reshape(sequence_count, KEY_VALUE_HEADS, group * token_span, HEAD_SIZE)

    def from_heads(value):
        value = value.reshape(sequence_count, KEY_VALUE_HEADS, group, token_span, HEAD_SIZE)
        return value.transpose(0, 3, 1, 2, 4).reshape(token_rows, q_width)

    score_scale = 1.0 / math.sqrt(HEAD_SIZE)
    q_heads = to_heads(query_rows)
    mask = jnp.concatenate([allowed] * group, axis=1)[:, None]
    scores = jnp.einsum("shqd,shkd->shqk", q_heads, k_all, preferred_element_type=f32)
    scores = jnp.where(mask, scores * score_scale, masked_score)
    top = jnp.max(scores, axis=-1, keepdims=True)
    expo = jnp.exp(scores - top)
    probs = expo / jnp.sum(expo, axis=-1, keepdims=True)
    probs_low = probs.astype(bf16)
    mixed = jnp.einsum("shqk,shkd->shqd", probs_low, v_all, preferred_element_type=f32)
    mixed_low = from_heads(mixed.astype(bf16))

    middle = inputs + order(dot(mixed_low, out_own), dot(mixed_low, out_par))
    normed_two = rms_scale(middle, gain_two).astype(bf16)
    both_own, both_par = dot(normed_two, gu_own), dot(normed_two, gu_par)
    ff_half = both_own.shape[1] // 2

    def hidden_of(both):
        return swiglu(both[:, :ff_half], both[:, ff_half:])

    hidden_own, hidden_back_own = jax.vjp(hidden_of, both_own)
    hidden_par, hidden_back_par = jax.vjp(hidden_of, both_par)
    hidden = order(hidden_own.astype(bf16), hidden_par.astype(bf16))
    result = (middle + order(dot(hidden, down_own), dot(hidden, down_par))).astype(bf16)

    grad_ff = cotangent.reshape(token_rows, width)
    grad_out = grad_ff.astype(f32)
    gff_own, gff_par = halves(grad_ff)
    s_down = scatter(dot_tn(hidden, gff_own), dot_tn(hidden, gff_par))
    d_hidden = dot_nt(gff_own, down_own) + dot_nt(gff_par, down_par)
    dh_own, dh_par = halves(d_hidden)
    d_both_own = hidden_back_own(dh_own)[0].astype(bf16)
    d_both_par = hidden_back_par(dh_par)[0].astype(bf16)
    s_gu = scatter(dot_tn(normed_two, d_both_own), dot_tn(normed_two, d_both_par))
    d_normed_two = dot_nt(d_both_own, gu_own) + dot_nt(d_both_par, gu_par)
    _, norm_two_back = jax.vjp(rms_scale, middle, gain_two)
    d_middle_norm, grad_two = norm_two_back(d_normed_two)
    d_middle = grad_out + d_middle_norm
    d_attn = d_middle.astype(bf16)
    da_own, da_par = halves(d_attn)
    s_out = scatter(dot_tn(mixed_low, da_own), dot_tn(mixed_low, da_par))
    d_mixed = (dot_nt(da_own, out_own) + dot_nt(da_par, out_par)).astype(bf16)
    g_heads = to_heads(d_mixed)

    d_probs = jnp.einsum("shqd,shkd->shqk", g_heads, v_all, preferred_element_type=f32)
    inner = jnp.sum(probs * d_probs, axis=-1, keepdims=True)
    d_scores = (probs * (d_probs - inner)).astype(bf16)
    d_queries = jnp.einsum("shqk,shkd->shqd", d_scores, k_all, preferred_element_type=f32)
    d_key = jnp.einsum("shqk,shqd->shkd", d_scores, q_heads, preferred_element_type=f32)
    d_value = jnp.einsum("shqk,shqd->shkd", probs_low, g_heads, preferred_element_type=f32)
    terms = jnp.stack([(d_key * score_scale).astype(bf16), d_value.astype(bf16)])
    terms = terms.reshape(
        2, sequence_count, KEY_VALUE_HEADS, 2 * z_count, token_span, HEAD_SIZE
    ).transpose(3, 0, 1, 2, 4, 5)
    terms_sum = (terms[:z_count].astype(f32) + swap(terms[z_count:]).astype(f32)).astype(bf16)
    d_kv = lax.psum_scatter(terms_sum, "z", scatter_dimension=0, tiled=False)
    d_kv = d_kv.transpose(0, 1, 3, 2, 4).astype(f32)
    d_queries = from_heads(d_queries * score_scale)

    _, query_back = jax.vjp(head_path, q_lin, gain_query)
    d_q_lin, grad_qnorm = query_back(d_queries.reshape(q_lin.shape))
    _, key_back = jax.vjp(head_path, key_linear, gain_key)
    d_k_lin, grad_knorm = key_back(d_kv[0].reshape(key_linear.shape))
    d_q_low = d_q_lin.reshape(token_rows, q_width).astype(bf16)
    d_k_low = d_k_lin.reshape(token_rows, kv_width).astype(bf16)
    d_v_low = d_kv[1].reshape(token_rows, kv_width).astype(bf16)
    split = [halves(d_q_low), halves(d_k_low), halves(d_v_low)]
    zeros = jnp.zeros((token_rows, 128), bf16)
    dl_own = jnp.concatenate([p[0] for p in split] + [zeros], axis=1)
    dl_par = jnp.concatenate([p[1] for p in split] + [zeros], axis=1)
    d_normed_one = dot_nt(dl_own, qkv_own) + dot_nt(dl_par, qkv_par)
    _, norm_one_back = jax.vjp(rms_scale, inputs, gain_one)
    d_input_norm, grad_one = norm_one_back(d_normed_one)
    input_grad = (d_middle + d_input_norm).reshape(sequence_count, token_span, width)

    grad_gains = jnp.concatenate([grad_one, grad_two, grad_qnorm, grad_knorm])
    grad_gains = grad_gains.reshape(chips, 2, share)

    def gain_block(part):
        block = jnp.pad(part[:, None, :], ((0, 0), (0, rows_chip - 1), (0, 128 - share)))
        return jnp.pad(block.reshape(width, 128), ((0, 0), (lin_width, 0)))

    gains_own = jnp.where(first_core, grad_gains[:, 0], grad_gains[:, 1])
    gains_par = jnp.where(first_core, grad_gains[:, 1], grad_gains[:, 0])
    s_qkv = scatter(
        dot_tn(first_normed, dl_own) + gain_block(gains_own),
        dot_tn(first_normed, dl_par) + gain_block(gains_par),
    )
    owned_gains = s_qkv[0, lin_width : lin_width + share].astype(f32)
    grad_query, grad_key, grad_value = own_rows(s_qkv[:, :lin_width], (half_q, half_kv, half_kv))
    (grad_output,) = own_rows(s_out, (width // 2,))
    grad_gate, grad_up = own_rows(s_gu, (ff_half, ff_half))
    (grad_down,) = own_rows(s_down, (width // 2,))
    return (
        result.reshape(sequence_count, token_span, width),
        input_grad,
        grad_query,
        grad_key,
        grad_value,
        grad_output,
        grad_gate,
        grad_up,
        grad_down,
        owned_gains,
    )


def solution(mesh):
    dp, ctx = mesh.devices.shape
    chips = Mesh(mesh.devices.reshape(dp, ctx // 2, 2), ("dp", "z", "core"))
    slots = ("z", "core")
    rows = P(("dp", "z", "core"), None)
    inner = jax.shard_map(
        local,
        mesh=chips,
        in_specs=(
            P("dp", slots, None),
            P("dp", slots, None),
            P("dp", None),
            P(),
            rows,
            rows,
            rows,
            rows,
            rows,
            rows,
            rows,
            P(("dp", "z", "core")),
        ),
        out_specs=(P("dp", slots, None), P("dp", slots, None))
        + (rows,) * 7
        + (P(("dp", "z", "core")),),
        check_vma=False,
    )
    return inner
```

```python
import math

import jax
import jax.numpy as jnp
from jax import lax
from jax.sharding import Mesh
from jax.sharding import PartitionSpec as P

QUERY_HEADS = 16
KEY_VALUE_HEADS = 8
HEAD_SIZE = 128


norm_eps = 1e-06
rope_base = 1000000.0
masked_score = -1e30


def rms_scale(value_rows, gain):
    return (
        value_rows
        * lax.rsqrt(jnp.mean(value_rows * value_rows, axis=-1, keepdims=True) + norm_eps)
        * gain
    )


def rotate(value_rows, positions):
    half = value_rows.shape[-1] // 2
    freq = rope_base ** (-(jnp.arange(half).astype(jnp.float32) * 2.0 / value_rows.shape[-1]))
    angle = positions.astype(jnp.float32)[:, None] * freq[None, :]
    cosine = jnp.cos(angle)[:, None, :]
    sine = jnp.sin(angle)[:, None, :]
    first_half = value_rows[..., :half]
    second_half = value_rows[..., half:]
    return jnp.concatenate(
        [first_half * cosine - second_half * sine, second_half * cosine + first_half * sine],
        axis=-1,
    )


def token_layout(segments, span_order, token_span):
    row_count, segment_length = segments.shape
    spots = jnp.arange(segment_length, dtype=jnp.int32)
    opens = jnp.concatenate(
        [jnp.ones((row_count, 1), dtype=jnp.bool_), segments[:, 1:] != segments[:, :-1]], axis=1
    )
    firsts = lax.cummax(jnp.where(opens, spots[None, :], jnp.int32(0)), axis=1)
    in_doc = spots[None, :] - firsts
    true_index = (
        span_order[:, None] * token_span + jnp.arange(token_span, dtype=jnp.int32)[None, :]
    ).reshape(segment_length)
    return (
        true_index,
        jnp.take(segments, true_index, axis=1),
        jnp.take(in_doc, true_index, axis=1),
    )


def swiglu(gate, up_part):
    return gate * jax.nn.sigmoid(gate) * up_part


SWAP = ((0, 1), (1, 0))


def swap(value):
    return lax.ppermute(value, "core", SWAP)


def local(
    tokens,
    cotangent,
    segments,
    span_order,
    w_query,
    key_weight,
    value_weight,
    w_output,
    w_gate,
    w_up,
    w_down,
    gains,
):
    sequence_count, token_span, width = tokens.shape
    token_rows = sequence_count * token_span
    group = QUERY_HEADS // KEY_VALUE_HEADS
    kv_width = KEY_VALUE_HEADS * HEAD_SIZE
    q_width = QUERY_HEADS * HEAD_SIZE
    core = lax.axis_index("core")
    first_core = core == 0
    chips = lax.axis_size("dp") * lax.axis_size("z")
    z_count = lax.axis_size("z")
    slot = lax.axis_index("z") * 2 + core
    f32, bf16 = jnp.float32, jnp.bfloat16

    def order(own, par, axis=-1):
        return jnp.concatenate(
            [jnp.where(first_core, own, par), jnp.where(first_core, par, own)], axis=axis
        )

    def halves(value):
        half = value.shape[-1] // 2
        a, b = value[..., :half], value[..., half:]
        return jnp.where(first_core, a, b), jnp.where(first_core, b, a)

    def chip_rows(parts):
        split = [halves(p) for p in parts]
        keep = jnp.concatenate([p[0] for p in split], axis=1)
        give = jnp.concatenate([p[1] for p in split], axis=1)
        return order(keep, swap(give), axis=0)

    def own_rows(value, sizes):
        rows = value.shape[0] // 2
        a, b = value[:rows], value[rows:]
        keep = jnp.where(first_core, a, b)
        got = swap(jnp.where(first_core, b, a))
        out, at = [], 0
        for size in sizes:
            out.append(order(keep[:, at : at + size], got[:, at : at + size]).astype(f32))
            at += size
        return out

    def shift_z(value, step):
        if step % z_count == 0:
            return value
        pairs = [(i, (i + step) % z_count) for i in range(z_count)]
        return lax.ppermute(value, "z", pairs)

    def fetch(value):
        return lax.all_gather(value, ("dp", "z"), axis=0, tiled=True)

    def gather(value):
        own = fetch(value)
        return own, swap(own)

    def scatter(own, par, before=None):
        total = (own + swap(par.astype(bf16)).astype(f32)).astype(bf16)
        if before is not None:
            total, _ = lax.optimization_barrier((total, before))
        return lax.psum_scatter(total, ("dp", "z"), scatter_dimension=0, tiled=True)

    def dot(a, b):
        return jnp.dot(a, b, preferred_element_type=f32)

    def dot_nt(a, b):
        return lax.dot_general(a, b, (((1,), (1,)), ((), ())), preferred_element_type=f32)

    def dot_tn(a, b):
        return lax.dot_general(a, b, (((0,), (0,)), ((), ())), preferred_element_type=f32)

    chip_qkv = chip_rows([w_query, key_weight, value_weight])
    chip_out = chip_rows([w_output])
    chip_gu = chip_rows([w_gate, w_up])
    chip_down = chip_rows([w_down])
    share = gains.shape[0]
    rows_chip = chip_qkv.shape[0]
    pad = jnp.pad(gains[None, :], ((0, rows_chip - 1), (0, 128 - share)))
    qkv_own, qkv_par = gather(jnp.concatenate([chip_qkv, pad], axis=1))
    lin_width = chip_qkv.shape[1]

    def gains_of(full):
        return full[::rows_chip, lin_width : lin_width + share]

    gain_all = order(gains_of(qkv_own)[:, None, :], gains_of(qkv_par)[:, None, :], axis=1)
    gain_all = gain_all.reshape(-1).astype(f32)
    gain_one = gain_all[:width]
    gain_two = gain_all[width : 2 * width]
    gain_query = gain_all[2 * width : 2 * width + HEAD_SIZE]
    gain_key = gain_all[2 * width + HEAD_SIZE :]

    true_index, seg_store, pos_store = token_layout(segments, span_order, token_span)
    query_index = lax.dynamic_slice_in_dim(true_index, slot * token_span, token_span, 0)
    query_segs = lax.dynamic_slice_in_dim(seg_store, slot * token_span, token_span, 1)
    query_pos = lax.dynamic_slice_in_dim(pos_store, slot * token_span, token_span, 1).reshape(
        token_rows
    )
    back = (lax.axis_index("z") - jnp.arange(z_count)) % z_count
    pairs_index = jnp.take(true_index.reshape(z_count, 2, token_span), back, axis=0)
    key_index = order(pairs_index[:, 0], pairs_index[:, 1], axis=0).reshape(-1)
    pairs_segs = seg_store.reshape(sequence_count, z_count, 2, token_span)
    pairs_segs = jnp.take(pairs_segs, back, axis=1)
    key_segs = order(pairs_segs[:, :, 0], pairs_segs[:, :, 1], axis=1).reshape(sequence_count, -1)
    allowed = (query_segs[:, :, None] == key_segs[:, None, :]) & (
        key_index[None, None, :] <= query_index[None, :, None]
    )

    def head_path(lin_part, gain):
        return rotate(rms_scale(lin_part, gain), query_pos)

    inputs = tokens.reshape(token_rows, width).astype(f32)
    first_normed = rms_scale(inputs, gain_one).astype(bf16)
    lin_own, lin_par = dot(first_normed, qkv_own), dot(first_normed, qkv_par)
    half_q, half_kv = q_width // 2, kv_width // 2

    def lin_slice(start, size):
        return order(lin_own[:, start : start + size], lin_par[:, start : start + size])

    q_lin = lin_slice(0, half_q).reshape(token_rows, QUERY_HEADS, HEAD_SIZE)
    key_linear = lin_slice(half_q, half_kv).reshape(token_rows, KEY_VALUE_HEADS, HEAD_SIZE)
    values_low = lin_slice(half_q + half_kv, half_kv).astype(bf16)
    query_rows = head_path(q_lin, gain_query).astype(bf16)
    keys = head_path(key_linear, gain_key).astype(bf16)

    kv = jnp.stack([keys.reshape(values_low.shape), values_low])
    kv = kv.reshape(2, sequence_count, token_span, KEY_VALUE_HEADS, HEAD_SIZE)
    kv = kv.transpose(0, 1, 3, 2, 4)
    kv_own = jnp.stack([shift_z(kv, step) for step in range(z_count)])
    kv_all = jnp.concatenate([kv_own, swap(kv_own)], axis=0)
    kv_all = kv_all.transpose(1, 2, 3, 0, 4, 5)
    key_count = kv_all.shape[3] * token_span
    kv_all = kv_all.reshape(2, sequence_count, KEY_VALUE_HEADS, key_count, HEAD_SIZE)
    k_all, v_all = kv_all[0], kv_all[1]

    out_own, out_par = gather(chip_out)
    gu_own, down_own = fetch(chip_gu), fetch(chip_down)

    def to_heads(value):
        value = value.reshape(sequence_count, token_span, KEY_VALUE_HEADS, group, HEAD_SIZE)
        value = value.transpose(0, 2, 3, 1, 4)
        return value.reshape(sequence_count, KEY_VALUE_HEADS, group * token_span, HEAD_SIZE)

    def from_heads(value):
        value = value.reshape(sequence_count, KEY_VALUE_HEADS, group, token_span, HEAD_SIZE)
        return value.transpose(0, 3, 1, 2, 4).reshape(token_rows, q_width)

    score_scale = 1.0 / math.sqrt(HEAD_SIZE)
    q_heads = to_heads(query_rows)
    mask = jnp.concatenate([allowed] * group, axis=1)[:, None]
    scores = jnp.einsum("shqd,shkd->shqk", q_heads, k_all, preferred_element_type=f32)
    scores = jnp.where(mask, scores * score_scale, masked_score)
    top = jnp.max(scores, axis=-1, keepdims=True)
    expo = jnp.exp(scores - top)
    probs = expo / jnp.sum(expo, axis=-1, keepdims=True)
    probs_low = probs.astype(bf16)
    mixed = jnp.einsum("shqk,shkd->shqd", probs_low, v_all, preferred_element_type=f32)
    mixed_low = from_heads(mixed.astype(bf16))
    mixed_low, gu_own, down_own = lax.optimization_barrier((mixed_low, gu_own, down_own))
    gu_par, down_par = swap(gu_own), swap(down_own)

    middle = inputs + order(dot(mixed_low, out_own), dot(mixed_low, out_par))
    normed_two = rms_scale(middle, gain_two).astype(bf16)
    both_own, both_par = dot(normed_two, gu_own), dot(normed_two, gu_par)
    ff_half = both_own.shape[1] // 2

    def hidden_of(both):
        return swiglu(both[:, :ff_half], both[:, ff_half:])

    hidden_own, hidden_back_own = jax.vjp(hidden_of, both_own)
    hidden_par, hidden_back_par = jax.vjp(hidden_of, both_par)
    hidden = order(hidden_own.astype(bf16), hidden_par.astype(bf16))
    result = (middle + order(dot(hidden, down_own), dot(hidden, down_par))).astype(bf16)

    grad_ff = cotangent.reshape(token_rows, width)
    grad_out = grad_ff.astype(f32)
    gff_own, gff_par = halves(grad_ff)
    s_down = scatter(dot_tn(hidden, gff_own), dot_tn(hidden, gff_par))
    d_hidden = dot_nt(gff_own, down_own) + dot_nt(gff_par, down_par)
    dh_own, dh_par = halves(d_hidden)
    d_both_own = hidden_back_own(dh_own)[0].astype(bf16)
    d_both_par = hidden_back_par(dh_par)[0].astype(bf16)
    s_gu = scatter(dot_tn(normed_two, d_both_own), dot_tn(normed_two, d_both_par), s_down)
    d_normed_two = dot_nt(d_both_own, gu_own) + dot_nt(d_both_par, gu_par)
    _, norm_two_back = jax.vjp(rms_scale, middle, gain_two)
    d_middle_norm, grad_two = norm_two_back(d_normed_two)
    d_middle = grad_out + d_middle_norm
    d_attn = d_middle.astype(bf16)
    da_own, da_par = halves(d_attn)
    s_out = scatter(dot_tn(mixed_low, da_own), dot_tn(mixed_low, da_par), s_gu)
    d_mixed = (dot_nt(da_own, out_own) + dot_nt(da_par, out_par)).astype(bf16)
    g_heads, s_down = lax.optimization_barrier((to_heads(d_mixed), s_down))

    d_probs = jnp.einsum("shqd,shkd->shqk", g_heads, v_all, preferred_element_type=f32)
    inner = jnp.sum(probs * d_probs, axis=-1, keepdims=True)
    d_scores = (probs * (d_probs - inner)).astype(bf16)
    d_queries = jnp.einsum("shqk,shkd->shqd", d_scores, k_all, preferred_element_type=f32)
    d_key = jnp.einsum("shqk,shqd->shkd", d_scores, q_heads, preferred_element_type=f32)
    d_value = jnp.einsum("shqk,shqd->shkd", probs_low, g_heads, preferred_element_type=f32)
    terms = jnp.stack([(d_key * score_scale).astype(bf16), d_value.astype(bf16)])
    terms = terms.reshape(
        2, sequence_count, KEY_VALUE_HEADS, 2 * z_count, token_span, HEAD_SIZE
    ).transpose(3, 0, 1, 2, 4, 5)
    terms_sum = terms[:z_count].astype(f32) + swap(terms[z_count:]).astype(f32)
    d_kv = terms_sum[0]
    for step in range(1, z_count):
        d_kv = d_kv + shift_z(terms_sum[step].astype(bf16), -step).astype(f32)
    d_kv, s_gu = lax.optimization_barrier((d_kv, s_gu))
    d_kv = d_kv.transpose(0, 1, 3, 2, 4)
    d_queries = from_heads(d_queries * score_scale)

    _, query_back = jax.vjp(head_path, q_lin, gain_query)
    d_q_lin, grad_qnorm = query_back(d_queries.reshape(q_lin.shape))
    _, key_back = jax.vjp(head_path, key_linear, gain_key)
    d_k_lin, grad_knorm = key_back(d_kv[0].reshape(key_linear.shape))
    d_q_low = d_q_lin.reshape(token_rows, q_width).astype(bf16)
    d_k_low = d_k_lin.reshape(token_rows, kv_width).astype(bf16)
    d_v_low = d_kv[1].reshape(token_rows, kv_width).astype(bf16)
    split = [halves(d_q_low), halves(d_k_low), halves(d_v_low)]
    zeros = jnp.zeros((token_rows, 128), bf16)
    dl_own = jnp.concatenate([p[0] for p in split] + [zeros], axis=1)
    dl_par = jnp.concatenate([p[1] for p in split] + [zeros], axis=1)
    d_normed_one = dot_nt(dl_own, qkv_own) + dot_nt(dl_par, qkv_par)
    _, norm_one_back = jax.vjp(rms_scale, inputs, gain_one)
    d_input_norm, grad_one = norm_one_back(d_normed_one)
    input_grad = (d_middle + d_input_norm).reshape(sequence_count, token_span, width)

    grad_gains = jnp.concatenate([grad_one, grad_two, grad_qnorm, grad_knorm])
    grad_gains = grad_gains.reshape(chips, 2, share)

    def gain_block(part):
        block = jnp.pad(part[:, None, :], ((0, 0), (0, rows_chip - 1), (0, 128 - share)))
        return jnp.pad(block.reshape(width, 128), ((0, 0), (lin_width, 0)))

    gains_own = jnp.where(first_core, grad_gains[:, 0], grad_gains[:, 1])
    gains_par = jnp.where(first_core, grad_gains[:, 1], grad_gains[:, 0])
    s_qkv = scatter(
        dot_tn(first_normed, dl_own) + gain_block(gains_own),
        dot_tn(first_normed, dl_par) + gain_block(gains_par),
    )
    owned_gains = s_qkv[0, lin_width : lin_width + share].astype(f32)
    grad_query, grad_key, grad_value = own_rows(s_qkv[:, :lin_width], (half_q, half_kv, half_kv))
    (grad_output,) = own_rows(s_out, (width // 2,))
    grad_gate, grad_up = own_rows(s_gu, (ff_half, ff_half))
    (grad_down,) = own_rows(s_down, (width // 2,))
    return (
        result.reshape(sequence_count, token_span, width),
        input_grad,
        grad_query,
        grad_key,
        grad_value,
        grad_output,
        grad_gate,
        grad_up,
        grad_down,
        owned_gains,
    )


def solution(mesh):
    dp, ctx = mesh.devices.shape
    chips = Mesh(mesh.devices.reshape(dp, ctx // 2, 2), ("dp", "z", "core"))
    slots = ("z", "core")
    rows = P(("dp", "z", "core"), None)
    inner = jax.shard_map(
        local,
        mesh=chips,
        in_specs=(
            P("dp", slots, None),
            P("dp", slots, None),
            P("dp", None),
            P(),
            rows,
            rows,
            rows,
            rows,
            rows,
            rows,
            rows,
            P(("dp", "z", "core")),
        ),
        out_specs=(P("dp", slots, None), P("dp", slots, None))
        + (rows,) * 7
        + (P(("dp", "z", "core")),),
        check_vma=False,
    )
    return inner
```
